512 devices in a mesh: blk: 32 (over y, x_lo, core), uly: 16 (over x_hi, z).
Axes of the slice: x: 4 (x_hi: 2, x_lo: 2; x = x_hi * 2 + x_lo), y: 8, z: 8, core: 2. Of those that a mesh axis runs over, the one named last changes fastest.
Arguments:
- query_states: bfloat16 [65536, 2048], P(('blk', 'uly')), may hold values from -16 to 16
- key_matrix: bfloat16 [65536, 512], P(('blk', 'uly')), may hold values from -16 to 16
- value_matrix: bfloat16 [65536, 512], P(('blk', 'uly')), may hold values from -6 to 6
- layer_output: bfloat16 [65536, 2048], P(('blk', 'uly')), may hold values from -4 to 4
- output_grad: bfloat16 [65536, 2048], P(('blk', 'uly')), may hold values from -6 to 6
- stretch_order: int32 [64], replicated, may hold values from 0 to 63, each once
- document_ids: int32 [65536], replicated, may hold values from 0 to 1023, never falling along the last dimension, each value on 1 to 128 neighbouring positions
Outputs:
- query_grad: bfloat16 [65536, 2048], P(('blk', 'uly'))
- key_grad: bfloat16 [65536, 512], P(('blk', 'uly'))
- value_grad: bfloat16 [65536, 512], P(('blk', 'uly'))
The draws below stay inside these ranges and needn't reach their ends.
Inputs may be any that keep to these rules, and one draw needn't show every extreme that they name: A permutation: each of 0 to 63 appears once; stored block c of 1024 rows holds the true positions stretch_order[c] * 1024 onward, in order. `document_ids`: never falling along the true positions; every document has 1 to 128 positions and one has exactly 128.
All inputs are finite; a program needn't handle non-finite values.
Results may differ from the reference program's by a relative error of at most 0.012.
Values may be sent and summed in bfloat16 or wider, within the bound.
A program may use at most 128 MiB of HBM per device.

```python
import math
import jax
import jax.numpy as jnp
import numpy as np
from jax import lax

QUERY_HEADS = 16
KEY_VALUE_HEADS = 4
HEAD_SIZE = 128
DOC_MOST = 128
SEQUENCE_TOKENS = 65536
STRETCHES = 64
DOCS = 1024


def draw_query_states(key, part):
    key = jax.random.fold_in(key, 7)
    leading_key = jax.random.fold_in(key, 0)
    final_result = jnp.clip(jax.random.normal(leading_key, (SEQUENCE_TOKENS, QUERY_HEADS, HEAD_SIZE), jnp.float32), -4.0, 4.0)
    return final_result.reshape(SEQUENCE_TOKENS, QUERY_HEADS * HEAD_SIZE).astype(jnp.bfloat16)


def draw_key_matrix(key, part):
    key = jax.random.fold_in(key, 13)
    leading_key = jax.random.fold_in(key, 0)
    final_result = jnp.clip(jax.random.normal(leading_key, (SEQUENCE_TOKENS, KEY_VALUE_HEADS, HEAD_SIZE), jnp.float32), -4.0, 4.0)
    return final_result.reshape(SEQUENCE_TOKENS, KEY_VALUE_HEADS * HEAD_SIZE).astype(jnp.bfloat16)


def shard_levels(stream_key, shape, cuts, smallest, top_value):
    gain, own = 1.0, jax.random.fold_in(stream_key, 6)
    for axis_at, parts in cuts:
        draws = jnp.exp(jax.random.uniform(jax.random.fold_in(own, axis_at), (parts,), jnp.float32, smallest / len(cuts), top_value / len(cuts)))
        gain = gain * jnp.repeat(draws, shape[axis_at] // parts).reshape([-1 if axis == axis_at else 1 for axis in range(len(shape))])
    return gain


def length_profile(amount, total, limit, skew):
    loads = [(1 << 20) // math.isqrt(standing ** skew) + 1 for standing in range(2, amount + 1)]
    rest, holding = total - limit - (amount - 1), [1] * (amount - 1)
    while rest > 0:
        movable = [i for i in range(amount - 1) if holding[i] < limit]
        mass, left = sum([loads[i] for i in movable]), rest
        for i in movable:
            more = min(limit - holding[i], max(1, left * loads[i] // mass), rest)
            holding[i] = holding[i] + more
            rest = rest - more
    return np.array([limit] + holding)


def ragged_sizes(rng, count, total, reach, lean):
    if count == 2:
        one = jax.random.randint(rng, (), max(1, total - reach), min(reach, total - 1) + 1)
        return jnp.stack([one, total - one])
    sizes = jnp.asarray(length_profile(count, total, reach, lean), jnp.int32)
    pairs = (count - 1) // 2
    giver, sink = sizes[1:1 + 2 * pairs:2], sizes[2:2 + 2 * pairs:2]
    room = jnp.minimum(giver - 1, reach - sink)
    moved = jax.random.randint(jax.random.fold_in(rng, 1), (pairs,), 0, 1 << 20) % (room + 1)
    sizes = sizes.at[1:1 + 2 * pairs:2].set(giver - moved).at[2:2 + 2 * pairs:2].set(sink + moved)
    return sizes[jax.random.permutation(jax.random.fold_in(rng, 2), count)]


def bell_draw(rng, dims, scale, limit, pieces=(), held_as=jnp.bfloat16):
    drawn = jax.random.normal(rng, dims, jnp.float32) * scale
    if len(pieces) > 0:
        drawn = shard_levels(rng, dims, pieces, -0.22, 0.18) * drawn
    return jnp.clip(drawn, min=-limit, max=limit).astype(held_as)


def setup_inputs(seed: int = 0) -> dict:
    key_of = jax.random.split(jax.random.key(seed), 8)
    return {
        "query_states": draw_query_states(jax.random.fold_in(key_of[7], 71), 0),
        "key_matrix": draw_key_matrix(jax.random.fold_in(key_of[7], 71), 0),
        "value_matrix": bell_draw(key_of[2], (SEQUENCE_TOKENS, KEY_VALUE_HEADS * HEAD_SIZE), 1.0, 6.0, ((0, 512),)),
        "layer_output": bell_draw(key_of[3], (SEQUENCE_TOKENS, QUERY_HEADS * HEAD_SIZE), 0.5, 4.0, ((0, 512),)),
        "output_grad": bell_draw(key_of[4], (SEQUENCE_TOKENS, QUERY_HEADS * HEAD_SIZE), 1.0, 6.0, ((0, 512),)),
        "stretch_order": jax.random.permutation(key_of[5], STRETCHES).astype(jnp.int32),
        "document_ids": jnp.searchsorted(jnp.cumsum(ragged_sizes(key_of[6], DOCS, SEQUENCE_TOKENS, DOC_MOST, 2)), jnp.arange(SEQUENCE_TOKENS), side="right").astype(jnp.int32),
    }


NEGATIVE = -1e+30

def rounded(tensor):
    return lax.optimization_barrier(tensor.astype(jnp.bfloat16)).astype(jnp.float32)

def product(left, right):
    return jnp.dot(left, right, precision=lax.Precision.HIGHEST, preferred_element_type=jnp.float32)

def reference(query_states, key_matrix, value_matrix, layer_output, output_grad, stretch_order, document_ids):
    token_sequence = query_states.shape[0]
    stretches = stretch_order.shape[0]
    stretch_rows = token_sequence // stretches
    inverse = jnp.argsort(stretch_order).astype(jnp.int32)
    group_width = QUERY_HEADS // KEY_VALUE_HEADS
    softmax_scale = 1.0 / math.sqrt(HEAD_SIZE)
    block_rows = math.gcd(token_sequence, 256)
    reach_rows = DOC_MOST
    window_rows = block_rows + reach_rows

    def actual_order(tensor, head_count):
        blocks = tensor.reshape(stretches, stretch_rows, head_count * HEAD_SIZE)[inverse]
        return jnp.transpose(blocks.reshape(token_sequence, head_count, HEAD_SIZE), (1, 0, 2)).astype(jnp.float32)

    def stored_order(heads):
        rows = jnp.transpose(heads, (1, 0, 2)).reshape(token_sequence, heads.shape[0] * HEAD_SIZE)
        return rows.reshape(stretches, stretch_rows, heads.shape[0] * HEAD_SIZE)[stretch_order].reshape(token_sequence, heads.shape[0] * HEAD_SIZE)
    query_heads = actual_order(query_states, QUERY_HEADS)
    key_head_split = jnp.repeat(actual_order(key_matrix, KEY_VALUE_HEADS), group_width, axis=0)
    value_head_split = jnp.repeat(actual_order(value_matrix, KEY_VALUE_HEADS), group_width, axis=0)
    output_heads = actual_order(layer_output, QUERY_HEADS)
    grad_heads = actual_order(output_grad, QUERY_HEADS)
    padding = jnp.zeros((reach_rows, HEAD_SIZE), jnp.float32)
    key_positions = jnp.arange(-reach_rows, token_sequence, dtype=jnp.int32)
    key_documents = jnp.concatenate([jnp.full((reach_rows,), -1, jnp.int32), document_ids.astype(jnp.int32)])
    query_positions = jnp.arange(token_sequence, dtype=jnp.int32)

    def one_head(inputs):
        query_head, key_head, value_head, output_head, grad_head = inputs
        grad_sum = lax.optimization_barrier(jnp.sum(grad_head * output_head, axis=1))
        key_padded = jnp.concatenate([padding, key_head], axis=0)
        value_padded = jnp.concatenate([padding, value_head], axis=0)

        def visit(totals, number):
            key_gradient_total, value_gradient_total = totals
            first_row = number * block_rows
            query_block = lax.dynamic_slice_in_dim(query_head, first_row, block_rows, 0)
            grad_block = lax.dynamic_slice_in_dim(grad_head, first_row, block_rows, 0)
            sum_block = lax.dynamic_slice_in_dim(grad_sum, first_row, block_rows, 0)
            position_block = lax.dynamic_slice_in_dim(query_positions, first_row, block_rows, 0)
            document_block = lax.dynamic_slice_in_dim(document_ids, first_row, block_rows, 0)
            key_block = lax.dynamic_slice_in_dim(key_padded, first_row, window_rows, 0)
            value_block = lax.dynamic_slice_in_dim(value_padded, first_row, window_rows, 0)
            key_position = lax.dynamic_slice_in_dim(key_positions, first_row, window_rows, 0)
            key_document = lax.dynamic_slice_in_dim(key_documents, first_row, window_rows, 0)
            visible = (key_position[None, :] <= position_block[:, None]) & (key_document[None, :] == document_block[:, None])
            logits = softmax_scale * product(query_block, key_block.T)
            masked = jnp.where(visible, logits, NEGATIVE)
            row_peak = lax.optimization_barrier(jnp.max(masked, axis=1))
            row_mass = lax.optimization_barrier(jnp.sum(jnp.where(visible, jnp.exp(masked - row_peak[:, None]), 0.0), axis=1))
            log_mass = row_peak + jnp.log(row_mass)
            probability = jnp.where(visible, jnp.exp(logits - log_mass[:, None]), 0.0)
            weight_grad = product(grad_block, value_block.T)
            slopes = rounded(probability * (weight_grad - sum_block[:, None]))
            query_block_grad = softmax_scale * product(slopes, key_block)
            key_window = lax.dynamic_slice_in_dim(key_gradient_total, first_row, window_rows, 0) + product(slopes.T, query_block)
            value_window = lax.dynamic_slice_in_dim(value_gradient_total, first_row, window_rows, 0) + product(rounded(probability).T, grad_block)
            key_gradient_total = lax.dynamic_update_slice_in_dim(key_gradient_total, key_window, first_row, 0)
            value_gradient_total = lax.dynamic_update_slice_in_dim(value_gradient_total, value_window, first_row, 0)
            return ((key_gradient_total, value_gradient_total), query_block_grad)
        zeros = jnp.zeros((token_sequence + reach_rows, HEAD_SIZE), jnp.float32)
        totals, query_grad = lax.scan(visit, (zeros, zeros), jnp.arange(token_sequence // block_rows, dtype=jnp.int32))
        return (query_grad.reshape(token_sequence, HEAD_SIZE), totals[0][reach_rows:], totals[1][reach_rows:])
    query_grad, key_gradient_total, value_gradient_total = lax.map(one_head, (query_heads, key_head_split, value_head_split, output_heads, grad_heads))
    query_out = stored_order(query_grad).astype(jnp.bfloat16)
    key_gradient_sum = (softmax_scale * key_gradient_total).reshape(KEY_VALUE_HEADS, group_width, token_sequence, HEAD_SIZE).sum(axis=1)
    value_gradient_sum = value_gradient_total.reshape(KEY_VALUE_HEADS, group_width, token_sequence, HEAD_SIZE).sum(axis=1)
    key_out = stored_order(key_gradient_sum).astype(jnp.bfloat16)
    value_out = stored_order(value_gradient_sum).astype(jnp.bfloat16)
    return (query_out, key_out, value_out)
```

```python
import functools
import math

import jax
import jax.numpy as jnp
from jax import lax
from jax.experimental import pallas as pl
from jax.experimental.pallas import tpu as pltpu
from jax.sharding import PartitionSpec as P

GROUPS = 4
WIDTH = 4
HEAD = 128
ROWS = 128
RUN = 8
STRETCHES = 64
SEQUENCE = STRETCHES * RUN * ROWS
TILE = 16
TILES = ROWS // TILE
NEGATIVE = -1e30
MESH = pl.DeviceIdType.MESH
F32 = jnp.float32
BF16 = jnp.bfloat16


def device_of(stretch, z):
    return (lax.div(stretch, 2), lax.rem(stretch, 2) * RUN + z)


def router_of(group, tile):
    y = lax.div(tile, 2)
    return y * 8 + lax.rem(tile, 2) * 4 + lax.rem(group - y + 8, 4)


def routed_by(stretch):
    y = lax.div(stretch, 8)
    tile = y * 2 + lax.rem(lax.div(stretch, 4), 2)
    return lax.rem(stretch + y, 4), lax.div(tile, TILES), lax.rem(tile, TILES)


def rows_of(tile):
    return pl.ds(pl.multiple_of(tile * TILE, TILE), TILE)


def columns_of(group):
    return pl.ds(pl.multiple_of(group * HEAD, HEAD), HEAD)


def as_column(row):
    n = row.shape[1]
    same = lax.broadcasted_iota(jnp.int32, (n, n), 0) == lax.broadcasted_iota(jnp.int32, (n, n), 1)
    spread = jnp.broadcast_to(row.astype(F32), (n, n))
    return jnp.sum(jnp.where(same, spread, 0.0), axis=1, keepdims=True)


def number_in(table, line, stretch):
    return jnp.clip(table[line, stretch], 0, STRETCHES - 1)


def wait_bytes(ref, sem):
    pltpu.make_async_copy(ref, ref, sem).wait()


def kernel(
    order, document_ids, query, key, value, layer_output, output_grad,
    dq, dk, dv,
    documents, q, o, do, k, v, own, before, back, returned, arrived, routed, arrived_back,
    routed_back, table, table_smem,
    in_sem, table_sem, kv_send, kv_recv, route_sem, route_send, back_send,
    route_back_sem, route_back_send, back_recv,
):
    blk, uly = lax.axis_index("blk"), lax.axis_index("uly")
    z = lax.rem(uly, RUN)
    me = blk * 2 + lax.div(uly, RUN)
    first, last = z == 0, z == RUN - 1
    group_here, kind_here, tile_here = routed_by(me)
    softmax_scale = 1.0 / math.sqrt(HEAD)

    loads = [
        pltpu.make_async_copy(source, target, in_sem.at[i])
        for i, (source, target) in enumerate(
            (
                (document_ids, documents),
                (key, k),
                (query, q),
                (value, v),
                (output_grad, do),
                (layer_output, o),
            )
        )
    ]
    for load in loads:
        load.start()

    barrier = pltpu.get_barrier_semaphore()

    def greet(stretch, at):
        pl.semaphore_signal(barrier, inc=1, device_id=device_of(stretch, at), device_id_type=MESH)

    @pl.when(first)
    def _():
        def to_last(i, carry):
            greet(i, RUN - 1)
            return carry

        def to_first(i, carry):
            greet(lax.rem(me + 1 + i, STRETCHES), 0)
            return carry

        lax.fori_loop(0, STRETCHES, to_last, 0)
        lax.fori_loop(0, STRETCHES - 1, to_first, 0)
        greet(me, 1)
        pl.semaphore_wait(barrier, STRETCHES)

    @pl.when(last)
    def _():
        greet(me, RUN - 2)
        pl.semaphore_wait(barrier, STRETCHES + 1)

    @pl.when(jnp.logical_not(first | last))
    def _():
        greet(me, z - 1)
        greet(me, z + 1)
        pl.semaphore_wait(barrier, 2)

    @pl.when(jnp.logical_not(last))
    def _():
        for group in range(GROUPS):
            for kind, source in enumerate((key, value)):
                pltpu.make_async_remote_copy(
                    source.at[:, pl.ds(group * HEAD, HEAD)],
                    before.at[group, kind],
                    kv_send,
                    kv_recv.at[group],
                    device_id=device_of(me, z + 1),
                    device_id_type=MESH,
                ).start()

    @pl.when(last)
    def _():
        def send(i, carry):
            group, tile = lax.div(i, TILES), lax.rem(i, TILES)
            for kind, source in enumerate((key, value)):
                pltpu.make_async_remote_copy(
                    source.at[rows_of(tile), columns_of(group)],
                    arrived.at[me],
                    kv_send,
                    route_sem,
                    device_id=device_of(router_of(group, kind * TILES + tile), 0),
                    device_id_type=MESH,
                ).start()
            return carry

        lax.fori_loop(0, GROUPS * TILES, send, 0)

    @pl.when(first | last)
    def _():
        lane = lax.broadcasted_iota(jnp.int32, (1, HEAD), 1)
        row = jnp.zeros((1, HEAD), jnp.int32)
        for stretch in range(STRETCHES):
            row = jnp.where(lane == stretch, order[stretch], row)
        previous = jnp.where(row == 0, STRETCHES - 1, row - 1)
        following = jnp.where(row == STRETCHES - 1, 0, row + 1)
        for i, wanted in enumerate((previous, following)):
            found = jnp.zeros((1, HEAD), jnp.int32)
            for stretch in range(STRETCHES):
                found = jnp.where(wanted == order[stretch], stretch, found)
            table[i : i + 1, :] = found
        copy = pltpu.make_async_copy(table, table_smem, table_sem)
        copy.start()
        copy.wait()

    loads[0].wait()
    place = order[me] * RUN + z
    query_document = documents[pl.ds(place, 1), :]
    before_document = documents[pl.ds(jnp.maximum(place - 1, 0), 1), :]
    before_document = jnp.where(place == 0, -1, before_document)
    down = lax.broadcasted_iota(jnp.int32, (ROWS, ROWS), 0)
    across = lax.broadcasted_iota(jnp.int32, (ROWS, ROWS), 1)
    wanted = query_document.astype(F32)
    before_bias = jnp.where(as_column(before_document) == wanted, 0.0, NEGATIVE)
    own_bias = jnp.where(
        (as_column(query_document) == wanted) & (down <= across), 0.0, NEGATIVE
    )
    bias = jnp.concatenate([before_bias, own_bias], axis=0)
    bias = jnp.concatenate([bias] * WIDTH, axis=1)

    @pl.when(first)
    def _():
        wait_bytes(arrived, route_sem)

        def pass_on(i, carry):
            stretch = lax.rem(me + 1 + i, STRETCHES)
            routed[stretch] = arrived[number_in(table_smem, 0, stretch)]
            pltpu.make_async_remote_copy(
                routed.at[stretch],
                before.at[group_here, kind_here, rows_of(tile_here)],
                route_send,
                kv_recv.at[group_here],
                device_id=device_of(stretch, 0),
                device_id_type=MESH,
            ).start()
            return carry

        lax.fori_loop(0, STRETCHES - 1, pass_on, 0)
        routed[me] = arrived[number_in(table_smem, 0, me)]
        pltpu.make_async_copy(
            routed.at[me],
            before.at[group_here, kind_here, rows_of(tile_here)],
            kv_recv.at[group_here],
        ).start()

    for load in loads[1:]:
        load.wait()

    contract_features = (((1,), (1,)), ((), ()))
    contract_rows = (((0,), (0,)), ((), ()))
    minus_ones = jnp.full((2 * ROWS, HEAD), -1.0, BF16)
    for group in range(GROUPS):
        wait_bytes(before.at[group], kv_recv.at[group])
        columns = slice(group * HEAD, (group + 1) * HEAD)

        def heads(tensor):
            return jnp.concatenate(
                [
                    tensor[:, (group * WIDTH + h) * HEAD : (group * WIDTH + h + 1) * HEAD]
                    for h in range(WIDTH)
                ],
                axis=0,
            )

        keys = jnp.concatenate([before[group, 0], k[:, columns]], axis=0)
        values = jnp.concatenate([before[group, 1], v[:, columns]], axis=0)
        queries, grads = heads(q), heads(do)
        products = (grads.astype(F32) * heads(o).astype(F32)).astype(BF16)
        scores = lax.dot_general(keys, queries, contract_features, preferred_element_type=F32)
        scores = scores * (softmax_scale * math.log2(math.e)) + bias
        weights = jnp.exp2(scores - jnp.max(scores, axis=0, keepdims=True))
        probability = weights * (1.0 / jnp.sum(weights, axis=0, keepdims=True))
        centred = lax.dot_general(
            jnp.concatenate([values, minus_ones], axis=1),
            jnp.concatenate([grads, products], axis=1),
            contract_features,
            preferred_element_type=F32,
        )
        slopes = (probability * centred).astype(BF16)
        key_part = softmax_scale * jnp.dot(slopes, queries, preferred_element_type=F32)
        value_part = jnp.dot(probability.astype(BF16), grads, preferred_element_type=F32)
        back[group, 0] = key_part[:ROWS].astype(BF16)
        back[group, 1] = value_part[:ROWS].astype(BF16)

        @pl.when(first)
        def _():
            def send(tile, carry):
                for kind in range(2):
                    pltpu.make_async_remote_copy(
                        back.at[group, kind, rows_of(tile)],
                        arrived_back.at[me],
                        back_send,
                        route_back_sem,
                        device_id=device_of(router_of(group, kind * TILES + tile), RUN - 1),
                        device_id_type=MESH,
                    ).start()
                return carry

            lax.fori_loop(0, TILES, send, 0)

        @pl.when(jnp.logical_not(first))
        def _():
            pltpu.make_async_remote_copy(
                back.at[group],
                returned.at[group],
                back_send,
                back_recv.at[group],
                device_id=device_of(me, z - 1),
                device_id_type=MESH,
            ).start()

        own[group, 0] = key_part[ROWS:]
        own[group, 1] = value_part[ROWS:]
        query_part = softmax_scale * lax.dot_general(
            slopes, keys, contract_rows, preferred_element_type=F32
        )
        for h in range(WIDTH):
            head = group * WIDTH + h
            dq[:, head * HEAD : (head + 1) * HEAD] = query_part[h * ROWS : (h + 1) * ROWS].astype(
                BF16
            )

    @pl.when(last)
    def _():
        wait_bytes(arrived_back, route_back_sem)

        def pass_on(i, carry):
            stretch = lax.rem(me + 1 + i, STRETCHES)
            routed_back[stretch] = arrived_back[number_in(table_smem, 1, stretch)]
            pltpu.make_async_remote_copy(
                routed_back.at[stretch],
                returned.at[group_here, kind_here, rows_of(tile_here)],
                route_back_send,
                back_recv.at[group_here],
                device_id=device_of(stretch, RUN - 1),
                device_id_type=MESH,
            ).start()
            return carry

        lax.fori_loop(0, STRETCHES - 1, pass_on, 0)
        routed_back[me] = arrived_back[number_in(table_smem, 1, me)]
        pltpu.make_async_copy(
            routed_back.at[me],
            returned.at[group_here, kind_here, rows_of(tile_here)],
            back_recv.at[group_here],
        ).start()

    for group in range(GROUPS):
        wait_bytes(returned.at[group], back_recv.at[group])
        columns = slice(group * HEAD, (group + 1) * HEAD)
        dk[:, columns] = (own[group, 0] + returned[group, 0].astype(F32)).astype(BF16)
        dv[:, columns] = (own[group, 1] + returned[group, 1].astype(F32)).astype(BF16)

    wait_bytes(before, kv_send)
    wait_bytes(back, back_send)

    @pl.when(first)
    def _():
        wait_bytes(routed.at[pl.ds(0, STRETCHES - 1)], route_send)

    @pl.when(last)
    def _():
        wait_bytes(routed_back.at[pl.ds(0, STRETCHES - 1)], route_back_send)


def per_device(
    query_states, key_matrix, value_matrix, layer_output, output_grad, stretch_order, document_ids
):
    vmem = pl.BlockSpec(memory_space=pltpu.VMEM)
    hbm = pl.BlockSpec(memory_space=pltpu.HBM)
    wide, narrow = query_states.shape, key_matrix.shape
    halo = (GROUPS, 2, ROWS, HEAD)
    routes = (STRETCHES, TILE, HEAD)
    dma = pltpu.SemaphoreType.DMA
    return pl.pallas_call(
        kernel,
        out_shape=[
            jax.ShapeDtypeStruct(wide, BF16),
            jax.ShapeDtypeStruct(narrow, BF16),
            jax.ShapeDtypeStruct(narrow, BF16),
        ],
        in_specs=[pl.BlockSpec(memory_space=pltpu.SMEM)] + [hbm] * 6,
        out_specs=[vmem] * 3,
        scratch_shapes=[
            pltpu.VMEM((SEQUENCE // ROWS, ROWS), jnp.int32),
            pltpu.VMEM(wide, BF16),
            pltpu.VMEM(wide, BF16),
            pltpu.VMEM(wide, BF16),
            pltpu.VMEM(narrow, BF16),
            pltpu.VMEM(narrow, BF16),
            pltpu.VMEM(halo, F32),
            pltpu.VMEM(halo, BF16),
            pltpu.VMEM(halo, BF16),
            pltpu.VMEM(halo, BF16),
            pltpu.VMEM(routes, BF16),
            pltpu.VMEM(routes, BF16),
            pltpu.VMEM(routes, BF16),
            pltpu.VMEM(routes, BF16),
            pltpu.VMEM((8, 128), jnp.int32),
            pltpu.SMEM((8, 128), jnp.int32),
            dma((6,)),
            dma(()),
            dma(()),
            dma((GROUPS,)),
            dma(()),
            dma(()),
            dma(()),
            dma(()),
            dma(()),
            dma((GROUPS,)),
        ],
        compiler_params=pltpu.CompilerParams(
            collective_id=0, has_side_effects=True, vmem_limit_bytes=40 * 2**20
        ),
        cost_estimate=pl.CostEstimate(
            flops=671_000_000, bytes_accessed=2_700_000, transcendentals=524_288
        ),
    )(
        stretch_order,
        *(
            pltpu.with_memory_space_constraint(operand, pltpu.HBM)
            for operand in (
                document_ids.reshape(-1, ROWS),
                query_states,
                key_matrix,
                value_matrix,
                layer_output,
                output_grad,
            )
        ),
    )


def solution(mesh):
    rows = P(("blk", "uly"), None)
    return jax.shard_map(
        per_device,
        mesh=mesh,
        in_specs=(rows, rows, rows, rows, rows, P(), P()),
        out_specs=(rows, rows, rows),
        check_vma=False,
    )
```

```python
import functools
import math

import jax
import jax.numpy as jnp
from jax import lax
from jax.experimental import pallas as pl
from jax.experimental.pallas import tpu as pltpu
from jax.sharding import PartitionSpec as P

GROUPS = 4
WIDTH = 4
HEAD = 128
ROWS = 128
RUN = 8
STRETCHES = 64
SEQUENCE = STRETCHES * RUN * ROWS
TILE = 16
TILES = ROWS // TILE
Y_STEPS = (4, 1, 3, 7, 5, 2, 6, 0)
NEGATIVE = -1e30
MESH = pl.DeviceIdType.MESH
F32 = jnp.float32
BF16 = jnp.bfloat16


def device_of(stretch, z):
    return (lax.div(stretch, 2), lax.rem(stretch, 2) * RUN + z)


def place_of(stretch):
    x = 2 * lax.rem(stretch, 2) + lax.rem(lax.div(stretch, 4), 2)
    return lax.div(stretch, 8), x, lax.rem(lax.div(stretch, 2), 2)


def routed_by(stretch):
    y, x, core = place_of(stretch)
    return core * 2 + lax.rem(lax.div(x, 2) + y, 2), lax.rem(x, 2), y


def for_core(me, core, visit, but_own=False):
    y, x, _ = place_of(me)

    def at(y_step, x_step):
        there_y, there_x = lax.rem(y + y_step, 8), lax.rem(x + x_step, 4)
        visit(there_y * 8 + lax.rem(there_x, 2) * 4 + core * 2 + lax.div(there_x, 2))

    def column(i, carry):
        x_step = jnp.where(i == 0, 2, jnp.where(i == 1, 1, 3))
        for y_step in Y_STEPS:
            at(y_step, x_step)
        return carry

    lax.fori_loop(0, 3, column, 0)
    for y_step in Y_STEPS[:-1] if but_own else Y_STEPS:
        at(y_step, 0)


def for_others(me, visit):
    core = place_of(me)[2]
    for_core(me, 1 - core, visit)
    for_core(me, core, visit, but_own=True)


def rows_of(tile):
    return pl.ds(pl.multiple_of(tile * TILE, TILE), TILE)


def columns_of(group):
    return pl.ds(pl.multiple_of(group * HEAD, HEAD), HEAD)


def as_column(row):
    n = row.shape[1]
    same = lax.broadcasted_iota(jnp.int32, (n, n), 0) == lax.broadcasted_iota(jnp.int32, (n, n), 1)
    spread = jnp.broadcast_to(row.astype(F32), (n, n))
    return jnp.sum(jnp.where(same, spread, 0.0), axis=1, keepdims=True)


def number_in(table, line, stretch):
    return jnp.clip(table[line, stretch], 0, STRETCHES - 1)


def wait_bytes(ref, sem):
    pltpu.make_async_copy(ref, ref, sem).wait()


def kernel(
    stretch_order, document_ids, query, key, value, layer_output, output_grad,
    dq, dk, dv,
    order, documents, q, o, do, k, v, with_products, scores, centred, inverses, slopes, own, before, back, returned, arrived, routed, arrived_back,
    routed_back, table, table_smem,
    in_sem, table_sem, kv_send, kv_recv, route_sem, route_send, back_send,
    route_back_sem, route_back_send, back_recv,
):
    blk, uly = lax.axis_index("blk"), lax.axis_index("uly")
    z = lax.rem(uly, RUN)
    me = blk * 2 + lax.div(uly, RUN)
    first, last = z == 0, z == RUN - 1
    group_here, kind_here, tile_here = routed_by(me)
    softmax_scale = 1.0 / math.sqrt(HEAD)

    loads = [
        pltpu.make_async_copy(source, target, in_sem.at[i])
        for i, (source, target) in enumerate(
            (
                (stretch_order, order),
                (document_ids, documents),
                (key, k),
                (query, q),
                (value, v),
                (output_grad, do),
                (layer_output, o),
            )
        )
    ]
    for load in loads:
        load.start()

    barrier = pltpu.get_barrier_semaphore()

    def greet(stretch, at):
        pl.semaphore_signal(barrier, inc=1, device_id=device_of(stretch, at), device_id_type=MESH)

    @pl.when(first)
    def _():
        for core in range(2):
            for_core(me, core, lambda stretch: greet(stretch, RUN - 1))
        for_others(me, lambda stretch: greet(stretch, 0))
        greet(me, 1)
        pl.semaphore_wait(barrier, STRETCHES)

    @pl.when(last)
    def _():
        greet(me, RUN - 2)
        pl.semaphore_wait(barrier, STRETCHES + 1)

    @pl.when(jnp.logical_not(first | last))
    def _():
        greet(me, z - 1)
        greet(me, z + 1)
        pl.semaphore_wait(barrier, 2)

    @pl.when(jnp.logical_not(last))
    def _():
        for group in range(GROUPS):
            for kind, source in enumerate((key, value)):
                pltpu.make_async_remote_copy(
                    source.at[:, pl.ds(group * HEAD, HEAD)],
                    before.at[group, kind],
                    kv_send,
                    kv_recv.at[group],
                    device_id=device_of(me, z + 1),
                    device_id_type=MESH,
                ).start()

    @pl.when(last)
    def _():
        def send(stretch):
            group, kind, tile = routed_by(stretch)
            for i, source in enumerate((key, value)):

                @pl.when(kind == i)
                def _():
                    pltpu.make_async_remote_copy(
                        source.at[rows_of(tile), columns_of(group)],
                        arrived.at[me],
                        kv_send,
                        route_sem,
                        device_id=device_of(stretch, 0),
                        device_id_type=MESH,
                    ).start()

        for core in range(2):
            for_core(me, core, send)

    loads[0].wait()
    loads[1].wait()

    @pl.when(first | last)
    def _():
        lane = lax.broadcasted_iota(jnp.int32, (1, HEAD), 1)
        row = jnp.zeros((1, HEAD), jnp.int32)
        for stretch in range(STRETCHES):
            row = jnp.where(lane == stretch, order[stretch], row)
        previous = jnp.where(row == 0, STRETCHES - 1, row - 1)
        following = jnp.where(row == STRETCHES - 1, 0, row + 1)
        for i, wanted in enumerate((previous, following)):
            found = jnp.zeros((1, HEAD), jnp.int32)
            for stretch in range(STRETCHES):
                found = jnp.where(wanted == order[stretch], stretch, found)
            table[i : i + 1, :] = found
        copy = pltpu.make_async_copy(table, table_smem, table_sem)
        copy.start()
        copy.wait()

    place = order[me] * RUN + z
    query_document = documents[pl.ds(place, 1), :]
    before_document = documents[pl.ds(jnp.maximum(place - 1, 0), 1), :]
    before_document = jnp.where(place == 0, -1, before_document)
    down = lax.broadcasted_iota(jnp.int32, (ROWS, ROWS), 0)
    across = lax.broadcasted_iota(jnp.int32, (ROWS, ROWS), 1)
    wanted = query_document.astype(F32)
    before_bias = jnp.where(as_column(before_document) == wanted, 0.0, NEGATIVE)
    own_bias = jnp.where(
        (as_column(query_document) == wanted) & (down <= across), 0.0, NEGATIVE
    )
    before_bias = jnp.concatenate([before_bias] * WIDTH, axis=1)
    own_bias = jnp.concatenate([own_bias] * WIDTH, axis=1)

    @pl.when(first)
    def _():
        wait_bytes(arrived, route_sem)

        def pass_on(stretch):
            routed[stretch] = arrived[number_in(table_smem, 0, stretch)]
            pltpu.make_async_remote_copy(
                routed.at[stretch],
                before.at[group_here, kind_here, rows_of(tile_here)],
                route_send,
                kv_recv.at[group_here],
                device_id=device_of(stretch, 0),
                device_id_type=MESH,
            ).start()

        for_others(me, pass_on)
        routed[me] = arrived[number_in(table_smem, 0, me)]
        pltpu.make_async_copy(
            routed.at[me],
            before.at[group_here, kind_here, rows_of(tile_here)],
            kv_recv.at[group_here],
        ).start()

    for load in loads[2:]:
        load.wait()

    contract_features = (((1,), (1,)), ((), ()))
    contract_rows = (((0,), (0,)), ((), ()))
    minus_ones = jnp.full((ROWS, HEAD), -1.0, BF16)
    scale_2 = softmax_scale * math.log2(math.e)

    def heads(tensor, group):
        return jnp.concatenate(
            [
                tensor[:, (group * WIDTH + h) * HEAD : (group * WIDTH + h + 1) * HEAD]
                for h in range(WIDTH)
            ],
            axis=0,
        )

    def scores_of(keys, group, bias):
        product = lax.dot_general(
            keys, heads(q, group), contract_features, preferred_element_type=F32
        )
        return product * scale_2 + bias

    def centred_of(values, group):
        return lax.dot_general(
            jnp.concatenate([values, minus_ones], axis=1),
            with_products[group],
            contract_features,
            preferred_element_type=F32,
        )

    for group in range(GROUPS):
        columns = slice(group * HEAD, (group + 1) * HEAD)
        grads = heads(do, group)
        products = (grads.astype(F32) * heads(o, group).astype(F32)).astype(BF16)
        with_products[group] = jnp.concatenate([grads, products], axis=1)
        scores[group] = scores_of(k[:, columns], group, own_bias)
        centred[group] = centred_of(v[:, columns], group)

    for group in range(GROUPS):
        wait_bytes(before.at[group], kv_recv.at[group])
        before_scores = scores_of(before[group, 0], group, before_bias)
        own_scores = scores[group]
        peak = jnp.maximum(
            jnp.max(before_scores, axis=0, keepdims=True),
            jnp.max(own_scores, axis=0, keepdims=True),
        )
        before_weights = jnp.exp2(before_scores - peak)
        own_weights = jnp.exp2(own_scores - peak)
        scores[group] = own_weights
        inverse = 1.0 / (
            jnp.sum(before_weights, axis=0, keepdims=True)
            + jnp.sum(own_weights, axis=0, keepdims=True)
        )
        inverses[group : group + 1, :] = inverse
        probability = before_weights * inverse
        slope = (probability * centred_of(before[group, 1], group)).astype(BF16)
        slopes[group, :ROWS] = slope
        back[group, 0] = (
            softmax_scale * jnp.dot(slope, heads(q, group), preferred_element_type=F32)
        ).astype(BF16)
        back[group, 1] = jnp.dot(
            probability.astype(BF16), heads(do, group), preferred_element_type=F32
        ).astype(BF16)

        @pl.when(jnp.logical_not(first))
        def _():
            pltpu.make_async_remote_copy(
                back.at[group],
                returned.at[group],
                back_send,
                back_recv.at[group],
                device_id=device_of(me, z - 1),
                device_id_type=MESH,
            ).start()

        if group % 2 == 1:

            @pl.when(first)
            def _():
                def send(stretch):
                    there, kind, tile = routed_by(stretch)
                    pltpu.make_async_remote_copy(
                        back.at[there, kind, rows_of(tile)],
                        arrived_back.at[me],
                        back_send,
                        route_back_sem,
                        device_id=device_of(stretch, RUN - 1),
                        device_id_type=MESH,
                    ).start()

                for_core(me, group // 2, send)

    for group in range(GROUPS):
        columns = slice(group * HEAD, (group + 1) * HEAD)
        probability = scores[group] * inverses[group : group + 1, :]
        slope = (probability * centred[group]).astype(BF16)
        slopes[group, ROWS:] = slope
        own[group, 0] = softmax_scale * jnp.dot(slope, heads(q, group), preferred_element_type=F32)
        own[group, 1] = jnp.dot(
            probability.astype(BF16), heads(do, group), preferred_element_type=F32
        )
        keys = jnp.concatenate([before[group, 0], k[:, columns]], axis=0)
        query_part = softmax_scale * lax.dot_general(
            slopes[group], keys, contract_rows, preferred_element_type=F32
        )
        for h in range(WIDTH):
            head = group * WIDTH + h
            dq[:, head * HEAD : (head + 1) * HEAD] = query_part[h * ROWS : (h + 1) * ROWS].astype(
                BF16
            )

    @pl.when(last)
    def _():
        wait_bytes(arrived_back, route_back_sem)

        def pass_on(stretch):
            routed_back[stretch] = arrived_back[number_in(table_smem, 1, stretch)]
            pltpu.make_async_remote_copy(
                routed_back.at[stretch],
                returned.at[group_here, kind_here, rows_of(tile_here)],
                route_back_send,
                back_recv.at[group_here],
                device_id=device_of(stretch, RUN - 1),
                device_id_type=MESH,
            ).start()

        for_others(me, pass_on)
        routed_back[me] = arrived_back[number_in(table_smem, 1, me)]
        pltpu.make_async_copy(
            routed_back.at[me],
            returned.at[group_here, kind_here, rows_of(tile_here)],
            back_recv.at[group_here],
        ).start()

    for group in range(GROUPS):
        wait_bytes(returned.at[group], back_recv.at[group])
        columns = slice(group * HEAD, (group + 1) * HEAD)
        dk[:, columns] = (own[group, 0] + returned[group, 0].astype(F32)).astype(BF16)
        dv[:, columns] = (own[group, 1] + returned[group, 1].astype(F32)).astype(BF16)

    wait_bytes(before, kv_send)
    wait_bytes(back, back_send)

    @pl.when(first)
    def _():
        wait_bytes(routed.at[pl.ds(0, STRETCHES - 1)], route_send)

    @pl.when(last)
    def _():
        wait_bytes(routed_back.at[pl.ds(0, STRETCHES - 1)], route_back_send)


def store(dq, dk, dv, query_grad, key_grad, value_grad, sem):
    copies = [
        pltpu.make_async_copy(source, target, sem.at[i])
        for i, (source, target) in enumerate(((dq, query_grad), (dk, key_grad), (dv, value_grad)))
    ]
    for copy in copies:
        copy.start()
    for copy in copies:
        copy.wait()


def per_device(
    query_states, key_matrix, value_matrix, layer_output, output_grad, stretch_order, document_ids
):
    vmem = pl.BlockSpec(memory_space=pltpu.VMEM)
    hbm = pl.BlockSpec(memory_space=pltpu.HBM)
    wide, narrow = query_states.shape, key_matrix.shape
    halo = (GROUPS, 2, ROWS, HEAD)
    routes = (STRETCHES, TILE, HEAD)
    dma = pltpu.SemaphoreType.DMA
    grads = pl.pallas_call(
        kernel,
        out_shape=[
            pltpu.VMEM(wide, BF16),
            pltpu.VMEM(narrow, BF16),
            pltpu.VMEM(narrow, BF16),
        ],
        in_specs=[hbm] * 7,
        out_specs=[vmem] * 3,
        scratch_shapes=[
            pltpu.SMEM((STRETCHES,), jnp.int32),
            pltpu.VMEM((SEQUENCE // ROWS, ROWS), jnp.int32),
            pltpu.VMEM(wide, BF16),
            pltpu.VMEM(wide, BF16),
            pltpu.VMEM(wide, BF16),
            pltpu.VMEM(narrow, BF16),
            pltpu.VMEM(narrow, BF16),
            pltpu.VMEM((GROUPS, WIDTH * ROWS, 2 * HEAD), BF16),
            pltpu.VMEM((GROUPS, ROWS, WIDTH * ROWS), F32),
            pltpu.VMEM((GROUPS, ROWS, WIDTH * ROWS), F32),
            pltpu.VMEM((8, WIDTH * ROWS), F32),
            pltpu.VMEM((GROUPS, 2 * ROWS, WIDTH * ROWS), BF16),
            pltpu.VMEM(halo, F32),
            pltpu.VMEM(halo, BF16),
            pltpu.VMEM(halo, BF16),
            pltpu.VMEM(halo, BF16),
            pltpu.VMEM(routes, BF16),
            pltpu.VMEM(routes, BF16),
            pltpu.VMEM(routes, BF16),
            pltpu.VMEM(routes, BF16),
            pltpu.VMEM((8, 128), jnp.int32),
            pltpu.SMEM((8, 128), jnp.int32),
            dma((7,)),
            dma(()),
            dma(()),
            dma((GROUPS,)),
            dma(()),
            dma(()),
            dma(()),
            dma(()),
            dma(()),
            dma((GROUPS,)),
        ],
        compiler_params=pltpu.CompilerParams(
            collective_id=0, has_side_effects=True, vmem_limit_bytes=40 * 2**20
        ),
        cost_estimate=pl.CostEstimate(
            flops=671_000_000, bytes_accessed=2_700_000, transcendentals=524_288
        ),
    )(
        *(
            pltpu.with_memory_space_constraint(operand, pltpu.HBM)
            for operand in (
                stretch_order,
                document_ids.reshape(-1, ROWS),
                query_states,
                key_matrix,
                value_matrix,
                layer_output,
                output_grad,
            )
        ),
    )

    return pl.pallas_call(
        store,
        out_shape=[jax.ShapeDtypeStruct(grad.shape, BF16) for grad in grads],
        in_specs=[vmem] * 3,
        out_specs=[pl.BlockSpec(memory_space=pl.ANY)] * 3,
        scratch_shapes=[dma((3,))],
        compiler_params=pltpu.CompilerParams(vmem_limit_bytes=40 * 2**20),
    )(*[grad for grad in grads])


def solution(mesh):
    rows = P(("blk", "uly"), None)
    return jax.shard_map(
        per_device,
        mesh=mesh,
        in_specs=(rows, rows, rows, rows, rows, P(), P()),
        out_specs=(rows, rows, rows),
        check_vma=False,
    )
```

```python
import functools
import math

import jax
import jax.numpy as jnp
from jax import lax
from jax.experimental import pallas as pl
from jax.experimental.pallas import tpu as pltpu
from jax.sharding import PartitionSpec as P

GROUPS = 4
WIDTH = 4
HEAD = 128
ROWS = 128
RUN = 8
STRETCHES = 64
SEQUENCE = STRETCHES * RUN * ROWS
TILE = 16
TILES = ROWS // TILE
Y_STEPS = (4, 1, 3, 7, 5, 2, 6, 0)
NEGATIVE = -1e30
MESH = pl.DeviceIdType.MESH
F32 = jnp.float32
BF16 = jnp.bfloat16


def device_of(stretch, z):
    return (lax.div(stretch, 2), lax.rem(stretch, 2) * RUN + z)


def place_of(stretch):
    x = 2 * lax.rem(stretch, 2) + lax.rem(lax.div(stretch, 4), 2)
    return lax.div(stretch, 8), x, lax.rem(lax.div(stretch, 2), 2)


def routed_by(stretch):
    y, x, core = place_of(stretch)
    return core * 2 + lax.rem(lax.div(x, 2) + y, 2), lax.rem(x, 2), y


def for_core(me, core, visit, but_own=False):
    y, x, _ = place_of(me)

    def at(y_step, x_step):
        there_y, there_x = lax.rem(y + y_step, 8), lax.rem(x + x_step, 4)
        visit(there_y * 8 + lax.rem(there_x, 2) * 4 + core * 2 + lax.div(there_x, 2))

    def column(i, carry):
        x_step = jnp.where(i == 0, 2, jnp.where(i == 1, 1, 3))
        for y_step in Y_STEPS:
            at(y_step, x_step)
        return carry

    lax.fori_loop(0, 3, column, 0)
    for y_step in Y_STEPS[:-1] if but_own else Y_STEPS:
        at(y_step, 0)


def for_others(me, visit):
    core = place_of(me)[2]
    for_core(me, 1 - core, visit)
    for_core(me, core, visit, but_own=True)


def rows_of(tile):
    return pl.ds(pl.multiple_of(tile * TILE, TILE), TILE)


def columns_of(group):
    return pl.ds(pl.multiple_of(group * HEAD, HEAD), HEAD)


def as_column(row):
    n = row.shape[1]
    same = lax.broadcasted_iota(jnp.int32, (n, n), 0) == lax.broadcasted_iota(jnp.int32, (n, n), 1)
    spread = jnp.broadcast_to(row.astype(F32), (n, n))
    return jnp.sum(jnp.where(same, spread, 0.0), axis=1, keepdims=True)


def number_in(table, line, stretch):
    return jnp.clip(table[line, stretch], 0, STRETCHES - 1)


def wait_bytes(ref, sem):
    pltpu.make_async_copy(ref, ref, sem).wait()


def kernel(
    stretch_order, document_ids, query, key, value, layer_output, output_grad,
    dq, dk, dv,
    order, documents, q, o, do, k, v, with_products, scores, centred, inverses, slopes, own, before, back, returned, arrived, routed, arrived_back,
    routed_back, table, table_smem,
    in_sem, table_sem, kv_send, kv_recv, route_sem, route_send, back_send,
    route_back_sem, route_back_send, back_recv,
):
    blk, uly = lax.axis_index("blk"), lax.axis_index("uly")
    z = lax.rem(uly, RUN)
    me = blk * 2 + lax.div(uly, RUN)
    first, last = z == 0, z == RUN - 1
    group_here, kind_here, tile_here = routed_by(me)
    softmax_scale = 1.0 / math.sqrt(HEAD)

    loads = [
        pltpu.make_async_copy(source, target, in_sem.at[i])
        for i, (source, target) in enumerate(
            (
                (stretch_order, order),
                (document_ids, documents),
                (key, k),
                (query, q),
                (value, v),
                (output_grad, do),
                (layer_output, o),
            )
        )
    ]
    for load in loads:
        load.start()

    barrier = pltpu.get_barrier_semaphore()

    def greet(stretch, at):
        pl.semaphore_signal(barrier, inc=1, device_id=device_of(stretch, at), device_id_type=MESH)

    @pl.when(first)
    def _():
        for core in range(2):
            for_core(me, core, lambda stretch: greet(stretch, RUN - 1))
        for_others(me, lambda stretch: greet(stretch, 0))
        pl.semaphore_wait(barrier, STRETCHES)

    @pl.when(jnp.logical_not(first))
    def _():
        greet(me, z - 1)

    @pl.when(last)
    def _():
        pl.semaphore_wait(barrier, STRETCHES)

    @pl.when(jnp.logical_not(first | last))
    def _():
        pl.semaphore_wait(barrier, 1)

    @pl.when(jnp.logical_not(last))
    def _():
        for group in range(GROUPS):
            for kind, source in enumerate((key, value)):
                pltpu.make_async_remote_copy(
                    source.at[:, pl.ds(group * HEAD, HEAD)],
                    before.at[group, kind],
                    kv_send,
                    kv_recv.at[group],
                    device_id=device_of(me, z + 1),
                    device_id_type=MESH,
                ).start()

    @pl.when(last)
    def _():
        def send(stretch):
            group, kind, tile = routed_by(stretch)
            for i, source in enumerate((key, value)):

                @pl.when(kind == i)
                def _():
                    pltpu.make_async_remote_copy(
                        source.at[rows_of(tile), columns_of(group)],
                        arrived.at[me],
                        kv_send,
                        route_sem,
                        device_id=device_of(stretch, 0),
                        device_id_type=MESH,
                    ).start()

        for_core(me, 0, send)
        wait_bytes(before.at[pl.ds(0, GROUPS // 2)], kv_send)
        for_core(me, 1, send)

    loads[0].wait()
    loads[1].wait()

    @pl.when(first | last)
    def _():
        lane = lax.broadcasted_iota(jnp.int32, (1, HEAD), 1)
        row = jnp.zeros((1, HEAD), jnp.int32)
        for stretch in range(STRETCHES):
            row = jnp.where(lane == stretch, order[stretch], row)
        previous = jnp.where(row == 0, STRETCHES - 1, row - 1)
        following = jnp.where(row == STRETCHES - 1, 0, row + 1)
        for i, wanted in enumerate((previous, following)):
            found = jnp.zeros((1, HEAD), jnp.int32)
            for stretch in range(STRETCHES):
                found = jnp.where(wanted == order[stretch], stretch, found)
            table[i : i + 1, :] = found
        copy = pltpu.make_async_copy(table, table_smem, table_sem)
        copy.start()
        copy.wait()

    place = order[me] * RUN + z
    query_document = documents[pl.ds(place, 1), :]
    before_document = documents[pl.ds(jnp.maximum(place - 1, 0), 1), :]
    before_document = jnp.where(place == 0, -1, before_document)
    down = lax.broadcasted_iota(jnp.int32, (ROWS, ROWS), 0)
    across = lax.broadcasted_iota(jnp.int32, (ROWS, ROWS), 1)
    wanted = query_document.astype(F32)
    before_bias = jnp.where(as_column(before_document) == wanted, 0.0, NEGATIVE)
    own_bias = jnp.where(
        (as_column(query_document) == wanted) & (down <= across), 0.0, NEGATIVE
    )
    before_bias = jnp.concatenate([before_bias] * WIDTH, axis=1)
    own_bias = jnp.concatenate([own_bias] * WIDTH, axis=1)

    @pl.when(first)
    def _():
        wait_bytes(arrived, route_sem)

        def pass_on(stretch):
            routed[stretch] = arrived[number_in(table_smem, 0, stretch)]
            pltpu.make_async_remote_copy(
                routed.at[stretch],
                before.at[group_here, kind_here, rows_of(tile_here)],
                route_send,
                kv_recv.at[group_here],
                device_id=device_of(stretch, 0),
                device_id_type=MESH,
            ).start()

        for_others(me, pass_on)
        routed[me] = arrived[number_in(table_smem, 0, me)]
        pltpu.make_async_copy(
            routed.at[me],
            before.at[group_here, kind_here, rows_of(tile_here)],
            kv_recv.at[group_here],
        ).start()

    for load in loads[2:]:
        load.wait()

    contract_features = (((1,), (1,)), ((), ()))
    contract_rows = (((0,), (0,)), ((), ()))
    minus_ones = jnp.full((ROWS, HEAD), -1.0, BF16)
    scale_2 = softmax_scale * math.log2(math.e)

    def heads(tensor, group):
        return jnp.concatenate(
            [
                tensor[:, (group * WIDTH + h) * HEAD : (group * WIDTH + h + 1) * HEAD]
                for h in range(WIDTH)
            ],
            axis=0,
        )

    def scores_of(keys, group, bias):
        product = lax.dot_general(
            keys, heads(q, group), contract_features, preferred_element_type=F32
        )
        return product * scale_2 + bias

    def centred_of(values, group):
        return lax.dot_general(
            jnp.concatenate([values, minus_ones], axis=1),
            with_products[group],
            contract_features,
            preferred_element_type=F32,
        )

    for group in range(GROUPS):
        columns = slice(group * HEAD, (group + 1) * HEAD)
        grads = heads(do, group)
        products = (grads.astype(F32) * heads(o, group).astype(F32)).astype(BF16)
        with_products[group] = jnp.concatenate([grads, products], axis=1)
        scores[group] = scores_of(k[:, columns], group, own_bias)
        centred[group] = centred_of(v[:, columns], group)

    for group in range(GROUPS):
        wait_bytes(before.at[group], kv_recv.at[group])
        before_scores = scores_of(before[group, 0], group, before_bias)
        own_scores = scores[group]
        peak = jnp.maximum(
            jnp.max(before_scores, axis=0, keepdims=True),
            jnp.max(own_scores, axis=0, keepdims=True),
        )
        before_weights = jnp.exp2(before_scores - peak)
        own_weights = jnp.exp2(own_scores - peak)
        scores[group] = own_weights
        inverse = 1.0 / (
            jnp.sum(before_weights, axis=0, keepdims=True)
            + jnp.sum(own_weights, axis=0, keepdims=True)
        )
        inverses[group : group + 1, :] = inverse
        probability = before_weights * inverse
        slope = (probability * centred_of(before[group, 1], group)).astype(BF16)
        slopes[group, :ROWS] = slope
        back[group, 0] = (
            softmax_scale * jnp.dot(slope, heads(q, group), preferred_element_type=F32)
        ).astype(BF16)
        back[group, 1] = jnp.dot(
            probability.astype(BF16), heads(do, group), preferred_element_type=F32
        ).astype(BF16)

        @pl.when(jnp.logical_not(first))
        def _():
            pltpu.make_async_remote_copy(
                back.at[group],
                returned.at[group],
                back_send,
                back_recv.at[group],
                device_id=device_of(me, z - 1),
                device_id_type=MESH,
            ).start()

        if group % 2 == 1:

            @pl.when(first)
            def _():
                def send(stretch):
                    there, kind, tile = routed_by(stretch)
                    pltpu.make_async_remote_copy(
                        back.at[there, kind, rows_of(tile)],
                        arrived_back.at[me],
                        back_send,
                        route_back_sem,
                        device_id=device_of(stretch, RUN - 1),
                        device_id_type=MESH,
                    ).start()

                for_core(me, group // 2, send)

    for group in range(GROUPS):
        columns = slice(group * HEAD, (group + 1) * HEAD)
        probability = scores[group] * inverses[group : group + 1, :]
        slope = (probability * centred[group]).astype(BF16)
        slopes[group, ROWS:] = slope
        own[group, 0] = softmax_scale * jnp.dot(slope, heads(q, group), preferred_element_type=F32)
        own[group, 1] = jnp.dot(
            probability.astype(BF16), heads(do, group), preferred_element_type=F32
        )
        keys = jnp.concatenate([before[group, 0], k[:, columns]], axis=0)
        query_part = softmax_scale * lax.dot_general(
            slopes[group], keys, contract_rows, preferred_element_type=F32
        )
        for h in range(WIDTH):
            head = group * WIDTH + h
            dq[:, head * HEAD : (head + 1) * HEAD] = query_part[h * ROWS : (h + 1) * ROWS].astype(
                BF16
            )

    @pl.when(last)
    def _():
        wait_bytes(arrived_back, route_back_sem)

        def pass_on(stretch):
            routed_back[stretch] = arrived_back[number_in(table_smem, 1, stretch)]
            pltpu.make_async_remote_copy(
                routed_back.at[stretch],
                returned.at[group_here, kind_here, rows_of(tile_here)],
                route_back_send,
                back_recv.at[group_here],
                device_id=device_of(stretch, RUN - 1),
                device_id_type=MESH,
            ).start()

        for_others(me, pass_on)
        routed_back[me] = arrived_back[number_in(table_smem, 1, me)]
        pltpu.make_async_copy(
            routed_back.at[me],
            returned.at[group_here, kind_here, rows_of(tile_here)],
            back_recv.at[group_here],
        ).start()

    for group in range(GROUPS):
        wait_bytes(returned.at[group], back_recv.at[group])
        columns = slice(group * HEAD, (group + 1) * HEAD)
        dk[:, columns] = (own[group, 0] + returned[group, 0].astype(F32)).astype(BF16)
        dv[:, columns] = (own[group, 1] + returned[group, 1].astype(F32)).astype(BF16)

    @pl.when(last)
    def _():
        wait_bytes(before.at[pl.ds(0, GROUPS // 2)], kv_send)

    @pl.when(jnp.logical_not(last))
    def _():
        wait_bytes(before, kv_send)

    wait_bytes(back, back_send)

    @pl.when(first)
    def _():
        wait_bytes(routed.at[pl.ds(0, STRETCHES - 1)], route_send)

    @pl.when(last)
    def _():
        wait_bytes(routed_back.at[pl.ds(0, STRETCHES - 1)], route_back_send)


def store(dq, dk, dv, query_grad, key_grad, value_grad, sem):
    copies = [
        pltpu.make_async_copy(source, target, sem.at[i])
        for i, (source, target) in enumerate(((dq, query_grad), (dk, key_grad), (dv, value_grad)))
    ]
    for copy in copies:
        copy.start()
    for copy in copies:
        copy.wait()


def per_device(
    query_states, key_matrix, value_matrix, layer_output, output_grad, stretch_order, document_ids
):
    vmem = pl.BlockSpec(memory_space=pltpu.VMEM)
    hbm = pl.BlockSpec(memory_space=pltpu.HBM)
    wide, narrow = query_states.shape, key_matrix.shape
    halo = (GROUPS, 2, ROWS, HEAD)
    routes = (STRETCHES, TILE, HEAD)
    dma = pltpu.SemaphoreType.DMA
    grads = pl.pallas_call(
        kernel,
        out_shape=[
            pltpu.VMEM(wide, BF16),
            pltpu.VMEM(narrow, BF16),
            pltpu.VMEM(narrow, BF16),
        ],
        in_specs=[hbm] * 7,
        out_specs=[vmem] * 3,
        scratch_shapes=[
            pltpu.SMEM((STRETCHES,), jnp.int32),
            pltpu.VMEM((SEQUENCE // ROWS, ROWS), jnp.int32),
            pltpu.VMEM(wide, BF16),
            pltpu.VMEM(wide, BF16),
            pltpu.VMEM(wide, BF16),
            pltpu.VMEM(narrow, BF16),
            pltpu.VMEM(narrow, BF16),
            pltpu.VMEM((GROUPS, WIDTH * ROWS, 2 * HEAD), BF16),
            pltpu.VMEM((GROUPS, ROWS, WIDTH * ROWS), F32),
            pltpu.VMEM((GROUPS, ROWS, WIDTH * ROWS), F32),
            pltpu.VMEM((8, WIDTH * ROWS), F32),
            pltpu.VMEM((GROUPS, 2 * ROWS, WIDTH * ROWS), BF16),
            pltpu.VMEM(halo, F32),
            pltpu.VMEM(halo, BF16),
            pltpu.VMEM(halo, BF16),
            pltpu.VMEM(halo, BF16),
            pltpu.VMEM(routes, BF16),
            pltpu.VMEM(routes, BF16),
            pltpu.VMEM(routes, BF16),
            pltpu.VMEM(routes, BF16),
            pltpu.VMEM((8, 128), jnp.int32),
            pltpu.SMEM((8, 128), jnp.int32),
            dma((7,)),
            dma(()),
            dma(()),
            dma((GROUPS,)),
            dma(()),
            dma(()),
            dma(()),
            dma(()),
            dma(()),
            dma((GROUPS,)),
        ],
        compiler_params=pltpu.CompilerParams(
            collective_id=0, has_side_effects=True, vmem_limit_bytes=40 * 2**20
        ),
        cost_estimate=pl.CostEstimate(
            flops=671_000_000, bytes_accessed=2_700_000, transcendentals=524_288
        ),
    )(
        *(
            pltpu.with_memory_space_constraint(operand, pltpu.HBM)
            for operand in (
                stretch_order,
                document_ids.reshape(-1, ROWS),
                query_states,
                key_matrix,
                value_matrix,
                layer_output,
                output_grad,
            )
        ),
    )

    return pl.pallas_call(
        store,
        out_shape=[jax.ShapeDtypeStruct(grad.shape, BF16) for grad in grads],
        in_specs=[vmem] * 3,
        out_specs=[pl.BlockSpec(memory_space=pl.ANY)] * 3,
        scratch_shapes=[dma((3,))],
        compiler_params=pltpu.CompilerParams(vmem_limit_bytes=40 * 2**20),
    )(*[grad for grad in grads])


def solution(mesh):
    rows = P(("blk", "uly"), None)
    return jax.shard_map(
        per_device,
        mesh=mesh,
        in_specs=(rows, rows, rows, rows, rows, P(), P()),
        out_specs=(rows, rows, rows),
        check_vma=False,
    )
```

```python
import functools
import math

import jax
import jax.numpy as jnp
from jax import lax
from jax.experimental import pallas as pl
from jax.experimental.pallas import tpu as pltpu
from jax.sharding import PartitionSpec as P

GROUPS = 4
WIDTH = 4
HEAD = 128
ROWS = 128
RUN = 8
STRETCHES = 64
SEQUENCE = STRETCHES * RUN * ROWS
TILE = 16
Y_STEPS = (4, 1, 3, 7, 5, 2, 6, 0)
NEGATIVE = -1e30
MESH = pl.DeviceIdType.MESH
F32 = jnp.float32
BF16 = jnp.bfloat16


def device_of(stretch, z):
    return (lax.div(stretch, 2), lax.rem(stretch, 2) * RUN + z)


def place_of(stretch):
    x = 2 * lax.rem(stretch, 2) + lax.rem(lax.div(stretch, 4), 2)
    return lax.div(stretch, 8), x, lax.rem(lax.div(stretch, 2), 2)


def routed_by(stretch):
    y, x, core = place_of(stretch)
    return core * 2 + lax.rem(lax.div(x, 2) + y, 2), lax.rem(x, 2), y


def for_core(me, core, visit, but_own=False):
    y, x, _ = place_of(me)

    def at(y_step, x_step):
        there_y, there_x = lax.rem(y + y_step, 8), lax.rem(x + x_step, 4)
        visit(there_y * 8 + lax.rem(there_x, 2) * 4 + core * 2 + lax.div(there_x, 2))

    def column(i, carry):
        x_step = jnp.where(i == 0, 2, jnp.where(i == 1, 1, 3))
        for y_step in Y_STEPS:
            at(y_step, x_step)
        return carry

    lax.fori_loop(0, 3, column, 0)
    for y_step in Y_STEPS[:-1] if but_own else Y_STEPS:
        at(y_step, 0)


def for_others(me, visit):
    core = place_of(me)[2]
    for_core(me, 1 - core, visit)
    for_core(me, core, visit, but_own=True)


def for_others_mixed(me, visit):
    step = 2 * (2 * place_of(me)[2] - 1)

    def both(stretch):
        visit(stretch)
        visit(stretch + step)

    for_core(me, 1 - place_of(me)[2], both, but_own=True)
    visit(me - step)


def rows_of(tile):
    return pl.ds(pl.multiple_of(tile * TILE, TILE), TILE)


def columns_of(group):
    return pl.ds(pl.multiple_of(group * HEAD, HEAD), HEAD)


def as_column(row):
    n = row.shape[1]
    same = lax.broadcasted_iota(jnp.int32, (n, n), 0) == lax.broadcasted_iota(jnp.int32, (n, n), 1)
    spread = jnp.broadcast_to(row.astype(F32), (n, n))
    return jnp.sum(jnp.where(same, spread, 0.0), axis=1, keepdims=True)


def number_in(table, line, stretch):
    return jnp.clip(table[line, stretch], 0, STRETCHES - 1)


def wait_bytes(ref, sem):
    pltpu.make_async_copy(ref, ref, sem).wait()


def kernel(
    stretch_order, document_ids, query, key, value, layer_output, output_grad,
    dq, dk, dv,
    order, documents, q, o, do, k, v, with_products, scores, centred, inverses, slopes, own, before, back, returned, arrived, routed, arrived_back,
    routed_back, table, table_smem,
    in_sem, table_sem, kv_send, kv_recv, route_sem, route_send, back_send,
    route_back_sem, route_back_send, back_recv,
):
    blk, uly = lax.axis_index("blk"), lax.axis_index("uly")
    z = lax.rem(uly, RUN)
    me = blk * 2 + lax.div(uly, RUN)
    first, last = z == 0, z == RUN - 1
    group_here, kind_here, tile_here = routed_by(me)
    softmax_scale = 1.0 / math.sqrt(HEAD)

    loads = [
        pltpu.make_async_copy(source, target, in_sem.at[i])
        for i, (source, target) in enumerate(
            (
                (stretch_order, order),
                (document_ids, documents),
                (key, k),
                (query, q),
                (value, v),
                (output_grad, do),
                (layer_output, o),
            )
        )
    ]
    @pl.when(jnp.logical_not(last))
    def _():
        for load in loads:
            load.start()

    barrier = pltpu.get_barrier_semaphore()

    def greet(stretch, at):
        pl.semaphore_signal(barrier, inc=1, device_id=device_of(stretch, at), device_id_type=MESH)

    @pl.when(first)
    def _():
        for core in range(2):
            for_core(me, core, lambda stretch: greet(stretch, RUN - 1))
        for_others(me, lambda stretch: greet(stretch, 0))
        pl.semaphore_wait(barrier, STRETCHES)

    @pl.when(jnp.logical_not(first))
    def _():
        greet(me, z - 1)

    @pl.when(last)
    def _():
        pl.semaphore_wait(barrier, STRETCHES)

    @pl.when(jnp.logical_not(first | last))
    def _():
        pl.semaphore_wait(barrier, 1)

    @pl.when(jnp.logical_not(last))
    def _():
        for group in range(GROUPS):
            for kind, source in enumerate((key, value)):
                pltpu.make_async_remote_copy(
                    source.at[:, pl.ds(group * HEAD, HEAD)],
                    before.at[group, kind],
                    kv_send,
                    kv_recv.at[group],
                    device_id=device_of(me, z + 1),
                    device_id_type=MESH,
                ).start()

    @pl.when(last)
    def _():
        def send(stretch):
            group, kind, tile = routed_by(stretch)
            for i, source in enumerate((key, value)):

                @pl.when(kind == i)
                def _():
                    pltpu.make_async_remote_copy(
                        source.at[rows_of(tile), columns_of(group)],
                        arrived.at[me],
                        kv_send,
                        route_sem,
                        device_id=device_of(stretch, 0),
                        device_id_type=MESH,
                    ).start()

        for_core(me, 0, send)
        wait_bytes(before.at[pl.ds(0, GROUPS // 2)], kv_send)
        for_core(me, 1, send)
        for load in loads:
            load.start()

    loads[0].wait()
    loads[1].wait()

    @pl.when(first | last)
    def _():
        lane = lax.broadcasted_iota(jnp.int32, (1, HEAD), 1)
        row = jnp.zeros((1, HEAD), jnp.int32)
        for stretch in range(STRETCHES):
            row = jnp.where(lane == stretch, order[stretch], row)
        previous = jnp.where(row == 0, STRETCHES - 1, row - 1)
        following = jnp.where(row == STRETCHES - 1, 0, row + 1)
        for i, wanted in enumerate((previous, following)):
            found = jnp.zeros((1, HEAD), jnp.int32)
            for stretch in range(STRETCHES):
                found = jnp.where(wanted == order[stretch], stretch, found)
            table[i : i + 1, :] = found
        copy = pltpu.make_async_copy(table, table_smem, table_sem)
        copy.start()
        copy.wait()

    place = order[me] * RUN + z
    query_document = documents[pl.ds(place, 1), :]
    before_document = documents[pl.ds(jnp.maximum(place - 1, 0), 1), :]
    before_document = jnp.where(place == 0, -1, before_document)
    down = lax.broadcasted_iota(jnp.int32, (ROWS, ROWS), 0)
    across = lax.broadcasted_iota(jnp.int32, (ROWS, ROWS), 1)
    wanted = query_document.astype(F32)
    before_bias = jnp.where(as_column(before_document) == wanted, 0.0, NEGATIVE)
    own_bias = jnp.where(
        (as_column(query_document) == wanted) & (down <= across), 0.0, NEGATIVE
    )
    before_bias = jnp.concatenate([before_bias] * WIDTH, axis=1)
    own_bias = jnp.concatenate([own_bias] * WIDTH, axis=1)

    for load in loads[2:]:
        load.wait()

    contract_features = (((1,), (1,)), ((), ()))
    contract_rows = (((0,), (0,)), ((), ()))
    minus_ones = jnp.full((ROWS, HEAD), -1.0, BF16)
    scale_2 = softmax_scale * math.log2(math.e)

    def heads(tensor, group):
        return jnp.concatenate(
            [
                tensor[:, (group * WIDTH + h) * HEAD : (group * WIDTH + h + 1) * HEAD]
                for h in range(WIDTH)
            ],
            axis=0,
        )

    def scores_of(keys, group, bias):
        product = lax.dot_general(
            keys, heads(q, group), contract_features, preferred_element_type=F32
        )
        return product * scale_2 + bias

    def centred_of(values, group):
        return lax.dot_general(
            jnp.concatenate([values, minus_ones], axis=1),
            with_products[group],
            contract_features,
            preferred_element_type=F32,
        )

    for group in range(GROUPS):
        columns = slice(group * HEAD, (group + 1) * HEAD)
        grads = heads(do, group)
        products = (grads.astype(F32) * heads(o, group).astype(F32)).astype(BF16)
        with_products[group] = jnp.concatenate([grads, products], axis=1)
        scores[group] = scores_of(k[:, columns], group, own_bias)
        centred[group] = centred_of(v[:, columns], group)

    @pl.when(first)
    def _():
        wait_bytes(arrived, route_sem)

        def pass_on(stretch):
            routed[stretch] = arrived[number_in(table_smem, 0, stretch)]
            pltpu.make_async_remote_copy(
                routed.at[stretch],
                before.at[group_here, kind_here, rows_of(tile_here)],
                route_send,
                kv_recv.at[group_here],
                device_id=device_of(stretch, 0),
                device_id_type=MESH,
            ).start()

        for_others(me, pass_on)
        routed[me] = arrived[number_in(table_smem, 0, me)]
        pltpu.make_async_copy(
            routed.at[me],
            before.at[group_here, kind_here, rows_of(tile_here)],
            kv_recv.at[group_here],
        ).start()

    for group in range(GROUPS):
        wait_bytes(before.at[group], kv_recv.at[group])
        before_scores = scores_of(before[group, 0], group, before_bias)
        own_scores = scores[group]
        peak = jnp.maximum(
            jnp.max(before_scores, axis=0, keepdims=True),
            jnp.max(own_scores, axis=0, keepdims=True),
        )
        before_weights = jnp.exp2(before_scores - peak)
        own_weights = jnp.exp2(own_scores - peak)
        scores[group] = own_weights
        inverse = 1.0 / (
            jnp.sum(before_weights, axis=0, keepdims=True)
            + jnp.sum(own_weights, axis=0, keepdims=True)
        )
        inverses[group : group + 1, :] = inverse
        probability = before_weights * inverse
        slope = (probability * centred_of(before[group, 1], group)).astype(BF16)
        slopes[group, :ROWS] = slope
        back[group, 0] = (
            softmax_scale * jnp.dot(slope, heads(q, group), preferred_element_type=F32)
        ).astype(BF16)
        back[group, 1] = jnp.dot(
            probability.astype(BF16), heads(do, group), preferred_element_type=F32
        ).astype(BF16)

        @pl.when(jnp.logical_not(first))
        def _():
            pltpu.make_async_remote_copy(
                back.at[group],
                returned.at[group],
                back_send,
                back_recv.at[group],
                device_id=device_of(me, z - 1),
                device_id_type=MESH,
            ).start()

        if group % 2 == 1:

            @pl.when(first)
            def _():
                def send(stretch):
                    there, kind, tile = routed_by(stretch)
                    pltpu.make_async_remote_copy(
                        back.at[there, kind, rows_of(tile)],
                        arrived_back.at[me],
                        back_send,
                        route_back_sem,
                        device_id=device_of(stretch, RUN - 1),
                        device_id_type=MESH,
                    ).start()

                for_core(me, group // 2, send)

    for group in range(GROUPS):
        columns = slice(group * HEAD, (group + 1) * HEAD)
        probability = scores[group] * inverses[group : group + 1, :]
        slope = (probability * centred[group]).astype(BF16)
        slopes[group, ROWS:] = slope
        own[group, 0] = softmax_scale * jnp.dot(slope, heads(q, group), preferred_element_type=F32)
        own[group, 1] = jnp.dot(
            probability.astype(BF16), heads(do, group), preferred_element_type=F32
        )
        keys = jnp.concatenate([before[group, 0], k[:, columns]], axis=0)
        query_part = softmax_scale * lax.dot_general(
            slopes[group], keys, contract_rows, preferred_element_type=F32
        )
        for h in range(WIDTH):
            head = group * WIDTH + h
            dq[:, head * HEAD : (head + 1) * HEAD] = query_part[h * ROWS : (h + 1) * ROWS].astype(
                BF16
            )

    @pl.when(last)
    def _():
        wait_bytes(arrived_back, route_back_sem)

        def pass_on(stretch):
            routed_back[stretch] = arrived_back[number_in(table_smem, 1, stretch)]
            pltpu.make_async_remote_copy(
                routed_back.at[stretch],
                returned.at[group_here, kind_here, rows_of(tile_here)],
                route_back_send,
                back_recv.at[group_here],
                device_id=device_of(stretch, RUN - 1),
                device_id_type=MESH,
            ).start()

        for_others_mixed(me, pass_on)
        routed_back[me] = arrived_back[number_in(table_smem, 1, me)]
        pltpu.make_async_copy(
            routed_back.at[me],
            returned.at[group_here, kind_here, rows_of(tile_here)],
            back_recv.at[group_here],
        ).start()

    for group in range(GROUPS):
        wait_bytes(returned.at[group], back_recv.at[group])
        columns = slice(group * HEAD, (group + 1) * HEAD)
        dk[:, columns] = (own[group, 0] + returned[group, 0].astype(F32)).astype(BF16)
        dv[:, columns] = (own[group, 1] + returned[group, 1].astype(F32)).astype(BF16)

    @pl.when(last)
    def _():
        wait_bytes(before.at[pl.ds(0, GROUPS // 2)], kv_send)

    @pl.when(jnp.logical_not(last))
    def _():
        wait_bytes(before, kv_send)

    wait_bytes(back, back_send)

    @pl.when(first)
    def _():
        wait_bytes(routed.at[pl.ds(0, STRETCHES - 1)], route_send)

    @pl.when(last)
    def _():
        wait_bytes(routed_back.at[pl.ds(0, STRETCHES - 1)], route_back_send)


def store(dq, dk, dv, query_grad, key_grad, value_grad, sem):
    copies = [
        pltpu.make_async_copy(source, target, sem.at[i])
        for i, (source, target) in enumerate(((dq, query_grad), (dk, key_grad), (dv, value_grad)))
    ]
    for copy in copies:
        copy.start()
    for copy in copies:
        copy.wait()


def per_device(
    query_states, key_matrix, value_matrix, layer_output, output_grad, stretch_order, document_ids
):
    vmem = pl.BlockSpec(memory_space=pltpu.VMEM)
    hbm = pl.BlockSpec(memory_space=pltpu.HBM)
    wide, narrow = query_states.shape, key_matrix.shape
    halo = (GROUPS, 2, ROWS, HEAD)
    routes = (STRETCHES, TILE, HEAD)
    dma = pltpu.SemaphoreType.DMA
    grads = pl.pallas_call(
        kernel,
        out_shape=[
            pltpu.VMEM(wide, BF16),
            pltpu.VMEM(narrow, BF16),
            pltpu.VMEM(narrow, BF16),
        ],
        in_specs=[hbm] * 7,
        out_specs=[vmem] * 3,
        scratch_shapes=[
            pltpu.SMEM((STRETCHES,), jnp.int32),
            pltpu.VMEM((SEQUENCE // ROWS, ROWS), jnp.int32),
            pltpu.VMEM(wide, BF16),
            pltpu.VMEM(wide, BF16),
            pltpu.VMEM(wide, BF16),
            pltpu.VMEM(narrow, BF16),
            pltpu.VMEM(narrow, BF16),
            pltpu.VMEM((GROUPS, WIDTH * ROWS, 2 * HEAD), BF16),
            pltpu.VMEM((GROUPS, ROWS, WIDTH * ROWS), F32),
            pltpu.VMEM((GROUPS, ROWS, WIDTH * ROWS), F32),
            pltpu.VMEM((8, WIDTH * ROWS), F32),
            pltpu.VMEM((GROUPS, 2 * ROWS, WIDTH * ROWS), BF16),
            pltpu.VMEM(halo, F32),
            pltpu.VMEM(halo, BF16),
            pltpu.VMEM(halo, BF16),
            pltpu.VMEM(halo, BF16),
            pltpu.VMEM(routes, BF16),
            pltpu.VMEM(routes, BF16),
            pltpu.VMEM(routes, BF16),
            pltpu.VMEM(routes, BF16),
            pltpu.VMEM((8, 128), jnp.int32),
            pltpu.SMEM((8, 128), jnp.int32),
            dma((7,)),
            dma(()),
            dma(()),
            dma((GROUPS,)),
            dma(()),
            dma(()),
            dma(()),
            dma(()),
            dma(()),
            dma((GROUPS,)),
        ],
        compiler_params=pltpu.CompilerParams(
            collective_id=0, has_side_effects=True, vmem_limit_bytes=40 * 2**20
        ),
        cost_estimate=pl.CostEstimate(
            flops=671_000_000, bytes_accessed=2_700_000, transcendentals=524_288
        ),
    )(
        *(
            pltpu.with_memory_space_constraint(operand, pltpu.HBM)
            for operand in (
                stretch_order,
                document_ids.reshape(-1, ROWS),
                query_states,
                key_matrix,
                value_matrix,
                layer_output,
                output_grad,
            )
        ),
    )

    return pl.pallas_call(
        store,
        out_shape=[jax.ShapeDtypeStruct(grad.shape, BF16) for grad in grads],
        in_specs=[vmem] * 3,
        out_specs=[pl.BlockSpec(memory_space=pl.ANY)] * 3,
        scratch_shapes=[dma((3,))],
        compiler_params=pltpu.CompilerParams(vmem_limit_bytes=40 * 2**20),
    )(*[grad for grad in grads])


def solution(mesh):
    rows = P(("blk", "uly"), None)
    return jax.shard_map(
        per_device,
        mesh=mesh,
        in_specs=(rows, rows, rows, rows, rows, P(), P()),
        out_specs=(rows, rows, rows),
        check_vma=False,
    )
```

```python
import functools
import math

import jax
import jax.numpy as jnp
from jax import lax
from jax.experimental import pallas as pl
from jax.experimental.pallas import tpu as pltpu
from jax.sharding import PartitionSpec as P

GROUPS = 4
WIDTH = 4
HEAD = 128
ROWS = 128
RUN = 8
STRETCHES = 64
SEQUENCE = STRETCHES * RUN * ROWS
TILE = 16
Y_STEPS = (4, 3, 5, 2, 6, 1, 7, 0)
NEGATIVE = -1e30
MESH = pl.DeviceIdType.MESH
F32 = jnp.float32
BF16 = jnp.bfloat16


def device_of(stretch, z):
    return (lax.div(stretch, 2), lax.rem(stretch, 2) * RUN + z)


def place_of(stretch):
    x = 2 * lax.rem(stretch, 2) + lax.rem(lax.div(stretch, 4), 2)
    return lax.div(stretch, 8), x, lax.rem(lax.div(stretch, 2), 2)


def routed_by(stretch):
    y, x, core = place_of(stretch)
    return core * 2 + lax.rem(lax.div(x, 2) + y, 2), lax.rem(x, 2), y


def for_core(me, core, visit, but_own=False):
    y, x, _ = place_of(me)

    def at(y_step, x_step):
        there_y, there_x = lax.rem(y + y_step, 8), lax.rem(x + x_step, 4)
        visit(there_y * 8 + lax.rem(there_x, 2) * 4 + core * 2 + lax.div(there_x, 2))

    def column(i, carry):
        x_step = jnp.where(i == 0, 2, jnp.where(i == 1, 1, 3))
        for y_step in Y_STEPS:
            at(y_step, x_step)
        return carry

    lax.fori_loop(0, 3, column, 0)
    for y_step in Y_STEPS[:-1] if but_own else Y_STEPS:
        at(y_step, 0)


def for_others(me, visit):
    core = place_of(me)[2]
    for_core(me, 1 - core, visit)
    for_core(me, core, visit, but_own=True)


def for_others_mixed(me, visit):
    step = 2 * (2 * place_of(me)[2] - 1)

    def both(stretch):
        visit(stretch)
        visit(stretch + step)

    for_core(me, 1 - place_of(me)[2], both, but_own=True)
    visit(me - step)


def rows_of(tile):
    return pl.ds(pl.multiple_of(tile * TILE, TILE), TILE)


def columns_of(group):
    return pl.ds(pl.multiple_of(group * HEAD, HEAD), HEAD)


def as_column(row):
    n = row.shape[1]
    same = lax.broadcasted_iota(jnp.int32, (n, n), 0) == lax.broadcasted_iota(jnp.int32, (n, n), 1)
    spread = jnp.broadcast_to(row.astype(F32), (n, n))
    return jnp.sum(jnp.where(same, spread, 0.0), axis=1, keepdims=True)


def number_in(table, line, stretch):
    return jnp.clip(table[line, stretch], 0, STRETCHES - 1)


def wait_bytes(ref, sem):
    pltpu.make_async_copy(ref, ref, sem).wait()


def kernel(
    stretch_order, document_ids, query, key, value, layer_output, output_grad,
    dq, dk, dv,
    order, documents, q, o, do, k, v, with_products, scores, centred, inverses, slopes, own, before, back, returned, arrived, routed, arrived_back,
    routed_back, table, table_smem,
    in_sem, table_sem, kv_send, kv_recv, route_sem, route_send, back_send,
    route_back_sem, route_back_send, back_recv,
):
    blk, uly = lax.axis_index("blk"), lax.axis_index("uly")
    z = lax.rem(uly, RUN)
    me = blk * 2 + lax.div(uly, RUN)
    first, last = z == 0, z == RUN - 1
    group_here, kind_here, tile_here = routed_by(me)
    softmax_scale = 1.0 / math.sqrt(HEAD)

    loads = [
        pltpu.make_async_copy(source, target, in_sem.at[i])
        for i, (source, target) in enumerate(
            (
                (stretch_order, order),
                (document_ids, documents),
                (key, k),
                (query, q),
                (value, v),
                (output_grad, do),
                (layer_output, o),
            )
        )
    ]
    @pl.when(jnp.logical_not(last))
    def _():
        for load in loads:
            load.start()

    barrier = pltpu.get_barrier_semaphore()

    def greet(stretch, at):
        pl.semaphore_signal(barrier, inc=1, device_id=device_of(stretch, at), device_id_type=MESH)

    @pl.when(first)
    def _():
        for core in range(2):
            for_core(me, core, lambda stretch: greet(stretch, RUN - 1))
        for_others(me, lambda stretch: greet(stretch, 0))
        pl.semaphore_wait(barrier, STRETCHES)

    @pl.when(jnp.logical_not(first))
    def _():
        greet(me, z - 1)

    @pl.when(last)
    def _():
        pl.semaphore_wait(barrier, STRETCHES)

    @pl.when(jnp.logical_not(first | last))
    def _():
        pl.semaphore_wait(barrier, 1)

    @pl.when(jnp.logical_not(last))
    def _():
        for group in range(GROUPS):
            for kind, source in enumerate((key, value)):
                pltpu.make_async_remote_copy(
                    source.at[:, pl.ds(group * HEAD, HEAD)],
                    before.at[group, kind],
                    kv_send,
                    kv_recv.at[group],
                    device_id=device_of(me, z + 1),
                    device_id_type=MESH,
                ).start()

    @pl.when(last)
    def _():
        def send(stretch):
            group, kind, tile = routed_by(stretch)
            for i, source in enumerate((key, value)):

                @pl.when(kind == i)
                def _():
                    pltpu.make_async_remote_copy(
                        source.at[rows_of(tile), columns_of(group)],
                        arrived.at[me],
                        kv_send,
                        route_sem,
                        device_id=device_of(stretch, 0),
                        device_id_type=MESH,
                    ).start()

        for_core(me, 0, send)
        wait_bytes(before.at[pl.ds(0, GROUPS // 2)], kv_send)
        for_core(me, 1, send)
        for load in loads:
            load.start()

    loads[0].wait()
    loads[1].wait()

    @pl.when(first | last)
    def _():
        lane = lax.broadcasted_iota(jnp.int32, (1, HEAD), 1)
        row = jnp.zeros((1, HEAD), jnp.int32)
        for stretch in range(STRETCHES):
            row = jnp.where(lane == stretch, order[stretch], row)
        previous = jnp.where(row == 0, STRETCHES - 1, row - 1)
        following = jnp.where(row == STRETCHES - 1, 0, row + 1)
        for i, wanted in enumerate((previous, following)):
            found = jnp.zeros((1, HEAD), jnp.int32)
            for stretch in range(STRETCHES):
                found = jnp.where(wanted == order[stretch], stretch, found)
            table[i : i + 1, :] = found
        copy = pltpu.make_async_copy(table, table_smem, table_sem)
        copy.start()
        copy.wait()

    place = order[me] * RUN + z
    query_document = documents[pl.ds(place, 1), :]
    before_document = documents[pl.ds(jnp.maximum(place - 1, 0), 1), :]
    before_document = jnp.where(place == 0, -1, before_document)
    down = lax.broadcasted_iota(jnp.int32, (ROWS, ROWS), 0)
    across = lax.broadcasted_iota(jnp.int32, (ROWS, ROWS), 1)
    wanted = query_document.astype(F32)
    before_bias = jnp.where(as_column(before_document) == wanted, 0.0, NEGATIVE)
    own_bias = jnp.where(
        (as_column(query_document) == wanted) & (down <= across), 0.0, NEGATIVE
    )
    before_bias = jnp.concatenate([before_bias] * WIDTH, axis=1)
    own_bias = jnp.concatenate([own_bias] * WIDTH, axis=1)

    for load in loads[2:]:
        load.wait()

    contract_features = (((1,), (1,)), ((), ()))
    contract_rows = (((0,), (0,)), ((), ()))
    minus_ones = jnp.full((ROWS, HEAD), -1.0, BF16)
    scale_2 = softmax_scale * math.log2(math.e)

    def heads(tensor, group):
        return jnp.concatenate(
            [
                tensor[:, (group * WIDTH + h) * HEAD : (group * WIDTH + h + 1) * HEAD]
                for h in range(WIDTH)
            ],
            axis=0,
        )

    def scores_of(keys, group, bias):
        product = lax.dot_general(
            keys, heads(q, group), contract_features, preferred_element_type=F32
        )
        return product * scale_2 + bias

    def centred_of(values, group):
        return lax.dot_general(
            jnp.concatenate([values, minus_ones], axis=1),
            with_products[group],
            contract_features,
            preferred_element_type=F32,
        )

    for group in range(GROUPS):
        columns = slice(group * HEAD, (group + 1) * HEAD)
        grads = heads(do, group)
        products = (grads.astype(F32) * heads(o, group).astype(F32)).astype(BF16)
        with_products[group] = jnp.concatenate([grads, products], axis=1)
        scores[group] = scores_of(k[:, columns], group, own_bias)
        centred[group] = centred_of(v[:, columns], group)

    @pl.when(first)
    def _():
        wait_bytes(arrived, route_sem)

        def pass_on(stretch):
            routed[stretch] = arrived[number_in(table_smem, 0, stretch)]
            pltpu.make_async_remote_copy(
                routed.at[stretch],
                before.at[group_here, kind_here, rows_of(tile_here)],
                route_send,
                kv_recv.at[group_here],
                device_id=device_of(stretch, 0),
                device_id_type=MESH,
            ).start()

        for_others(me, pass_on)
        routed[me] = arrived[number_in(table_smem, 0, me)]
        pltpu.make_async_copy(
            routed.at[me],
            before.at[group_here, kind_here, rows_of(tile_here)],
            kv_recv.at[group_here],
        ).start()

    for group in range(GROUPS):
        wait_bytes(before.at[group], kv_recv.at[group])
        before_scores = scores_of(before[group, 0], group, before_bias)
        own_scores = scores[group]
        peak = jnp.maximum(
            jnp.max(before_scores, axis=0, keepdims=True),
            jnp.max(own_scores, axis=0, keepdims=True),
        )
        before_weights = jnp.exp2(before_scores - peak)
        own_weights = jnp.exp2(own_scores - peak)
        scores[group] = own_weights
        inverse = 1.0 / (
            jnp.sum(before_weights, axis=0, keepdims=True)
            + jnp.sum(own_weights, axis=0, keepdims=True)
        )
        inverses[group : group + 1, :] = inverse
        probability = before_weights * inverse
        slope = (probability * centred_of(before[group, 1], group)).astype(BF16)
        slopes[group, :ROWS] = slope
        back[group, 0] = (
            softmax_scale * jnp.dot(slope, heads(q, group), preferred_element_type=F32)
        ).astype(BF16)
        back[group, 1] = jnp.dot(
            probability.astype(BF16), heads(do, group), preferred_element_type=F32
        ).astype(BF16)

        @pl.when(jnp.logical_not(first))
        def _():
            pltpu.make_async_remote_copy(
                back.at[group],
                returned.at[group],
                back_send,
                back_recv.at[group],
                device_id=device_of(me, z - 1),
                device_id_type=MESH,
            ).start()

        if group % 2 == 1:

            @pl.when(first)
            def _():
                def send(stretch):
                    there, kind, tile = routed_by(stretch)
                    pltpu.make_async_remote_copy(
                        back.at[there, kind, rows_of(tile)],
                        arrived_back.at[me],
                        back_send,
                        route_back_sem,
                        device_id=device_of(stretch, RUN - 1),
                        device_id_type=MESH,
                    ).start()

                for_core(me, group // 2, send)

    for group in range(GROUPS):
        columns = slice(group * HEAD, (group + 1) * HEAD)
        probability = scores[group] * inverses[group : group + 1, :]
        slope = (probability * centred[group]).astype(BF16)
        slopes[group, ROWS:] = slope
        own[group, 0] = softmax_scale * jnp.dot(slope, heads(q, group), preferred_element_type=F32)
        own[group, 1] = jnp.dot(
            probability.astype(BF16), heads(do, group), preferred_element_type=F32
        )
        keys = jnp.concatenate([before[group, 0], k[:, columns]], axis=0)
        query_part = softmax_scale * lax.dot_general(
            slopes[group], keys, contract_rows, preferred_element_type=F32
        )
        for h in range(WIDTH):
            head = group * WIDTH + h
            dq[:, head * HEAD : (head + 1) * HEAD] = query_part[h * ROWS : (h + 1) * ROWS].astype(
                BF16
            )

    @pl.when(last)
    def _():
        wait_bytes(arrived_back, route_back_sem)

        def pass_on(stretch):
            routed_back[stretch] = arrived_back[number_in(table_smem, 1, stretch)]
            pltpu.make_async_remote_copy(
                routed_back.at[stretch],
                returned.at[group_here, kind_here, rows_of(tile_here)],
                route_back_send,
                back_recv.at[group_here],
                device_id=device_of(stretch, RUN - 1),
                device_id_type=MESH,
            ).start()

        for_others_mixed(me, pass_on)
        routed_back[me] = arrived_back[number_in(table_smem, 1, me)]
        pltpu.make_async_copy(
            routed_back.at[me],
            returned.at[group_here, kind_here, rows_of(tile_here)],
            back_recv.at[group_here],
        ).start()

    for group in range(GROUPS):
        wait_bytes(returned.at[group], back_recv.at[group])
        columns = slice(group * HEAD, (group + 1) * HEAD)
        dk[:, columns] = (own[group, 0] + returned[group, 0].astype(F32)).astype(BF16)
        dv[:, columns] = (own[group, 1] + returned[group, 1].astype(F32)).astype(BF16)

    @pl.when(last)
    def _():
        wait_bytes(before.at[pl.ds(0, GROUPS // 2)], kv_send)

    @pl.when(jnp.logical_not(last))
    def _():
        wait_bytes(before, kv_send)

    wait_bytes(back, back_send)

    @pl.when(first)
    def _():
        wait_bytes(routed.at[pl.ds(0, STRETCHES - 1)], route_send)

    @pl.when(last)
    def _():
        wait_bytes(routed_back.at[pl.ds(0, STRETCHES - 1)], route_back_send)


def store(dq, dk, dv, query_grad, key_grad, value_grad, sem):
    copies = [
        pltpu.make_async_copy(source, target, sem.at[i])
        for i, (source, target) in enumerate(((dq, query_grad), (dk, key_grad), (dv, value_grad)))
    ]
    for copy in copies:
        copy.start()
    for copy in copies:
        copy.wait()


def per_device(
    query_states, key_matrix, value_matrix, layer_output, output_grad, stretch_order, document_ids
):
    vmem = pl.BlockSpec(memory_space=pltpu.VMEM)
    hbm = pl.BlockSpec(memory_space=pltpu.HBM)
    wide, narrow = query_states.shape, key_matrix.shape
    halo = (GROUPS, 2, ROWS, HEAD)
    routes = (STRETCHES, TILE, HEAD)
    dma = pltpu.SemaphoreType.DMA
    grads = pl.pallas_call(
        kernel,
        out_shape=[
            pltpu.VMEM(wide, BF16),
            pltpu.VMEM(narrow, BF16),
            pltpu.VMEM(narrow, BF16),
        ],
        in_specs=[hbm] * 7,
        out_specs=[vmem] * 3,
        scratch_shapes=[
            pltpu.SMEM((STRETCHES,), jnp.int32),
            pltpu.VMEM((SEQUENCE // ROWS, ROWS), jnp.int32),
            pltpu.VMEM(wide, BF16),
            pltpu.VMEM(wide, BF16),
            pltpu.VMEM(wide, BF16),
            pltpu.VMEM(narrow, BF16),
            pltpu.VMEM(narrow, BF16),
            pltpu.VMEM((GROUPS, WIDTH * ROWS, 2 * HEAD), BF16),
            pltpu.VMEM((GROUPS, ROWS, WIDTH * ROWS), F32),
            pltpu.VMEM((GROUPS, ROWS, WIDTH * ROWS), F32),
            pltpu.VMEM((8, WIDTH * ROWS), F32),
            pltpu.VMEM((GROUPS, 2 * ROWS, WIDTH * ROWS), BF16),
            pltpu.VMEM(halo, F32),
            pltpu.VMEM(halo, BF16),
            pltpu.VMEM(halo, BF16),
            pltpu.VMEM(halo, BF16),
            pltpu.VMEM(routes, BF16),
            pltpu.VMEM(routes, BF16),
            pltpu.VMEM(routes, BF16),
            pltpu.VMEM(routes, BF16),
            pltpu.VMEM((8, 128), jnp.int32),
            pltpu.SMEM((8, 128), jnp.int32),
            dma((7,)),
            dma(()),
            dma(()),
            dma((GROUPS,)),
            dma(()),
            dma(()),
            dma(()),
            dma(()),
            dma(()),
            dma((GROUPS,)),
        ],
        compiler_params=pltpu.CompilerParams(
            collective_id=0, has_side_effects=True, vmem_limit_bytes=40 * 2**20
        ),
        cost_estimate=pl.CostEstimate(
            flops=671_000_000, bytes_accessed=2_700_000, transcendentals=524_288
        ),
    )(
        *(
            pltpu.with_memory_space_constraint(operand, pltpu.HBM)
            for operand in (
                stretch_order,
                document_ids.reshape(-1, ROWS),
                query_states,
                key_matrix,
                value_matrix,
                layer_output,
                output_grad,
            )
        ),
    )

    return pl.pallas_call(
        store,
        out_shape=[jax.ShapeDtypeStruct(grad.shape, BF16) for grad in grads],
        in_specs=[vmem] * 3,
        out_specs=[pl.BlockSpec(memory_space=pl.ANY)] * 3,
        scratch_shapes=[dma((3,))],
        compiler_params=pltpu.CompilerParams(vmem_limit_bytes=40 * 2**20),
    )(*[grad for grad in grads])


def solution(mesh):
    rows = P(("blk", "uly"), None)
    return jax.shard_map(
        per_device,
        mesh=mesh,
        in_specs=(rows, rows, rows, rows, rows, P(), P()),
        out_specs=(rows, rows, rows),
        check_vma=False,
    )
```
